512 devices in a mesh: seq: 128 (over y, x_hi, z), scene: 4 (over x_lo, core).
Axes of the slice: x: 4 (x_hi: 2, x_lo: 2; x = x_hi * 2 + x_lo), y: 4, z: 16, core: 2. Of those that a mesh axis runs over, the one named last changes fastest.
Arguments:
- features: bfloat16 [131072, 1280], P(('scene', 'seq')), parts along dimension 0, may hold values from -6 to 6
- norm_gain: float32 [1280], replicated, may hold values from 0.1 to 1.9
- pred_weight: bfloat16 [1280, 1024], replicated, may hold values from -0.15625 to 0.15625
- target: bfloat16 [131072, 1024], P(('scene', 'seq')), parts along dimension 0, may hold values from -6 to 6
- patch_mask: int32 [131072], P(('scene', 'seq')), parts along dimension 0, may hold values 0 or 1
- band_level: int32 [16], replicated, may hold values from 1 to 16
Outputs:
- pixel_grad: float32 [131072, 1024], P(('scene', 'seq')), parts along dimension 0
- loss: float32 [4], P('scene'), parts along dimension 0
The draws below stay inside these ranges and needn't reach their ends.
There are 4 independent parts, one for each index of `scene`. The reference program is written for one: setup_inputs(seed, part) draws one part's arguments, and reference() takes and returns one part's arrays. A program takes and returns all parts, laid end to end along the dimension named above; an argument that names none is the same for every part. Nothing has to cross between parts.
All inputs are finite; a program needn't handle non-finite values. No bound on the sum of `patch_mask` on one device may be relied on, other than what follows from the above.
Results may differ from the reference program's by a relative error of at most 0.0017.
The reference program's roundings to bfloat16 on the way (of `normed`) count: a program that leaves them out, or rounds other values in their place, can miss the bound.
Values sent between devices are 32-bit elements; how exact they have to be, the bound alone decides.
A program may use at most 64 MiB of HBM per device.

```python
import jax
import jax.numpy as jnp
from jax import lax

D = 1280
PATCH = 16
CH = 4
W = 4096
NBIN = 16
PIX = 1024
PC = 256
H = 2048
TOKENS = 32768


def touch_ends(values, rng, low, high):
    longest = values.shape.index(max(values.shape))
    spots = []
    for shift in (0, 1):
        where = [jax.random.randint(jax.random.fold_in(rng, axis), (), 0, length) for axis, length in enumerate(values.shape)]
        where[longest] = (where[longest] + shift) % values.shape[longest]
        spots.append(tuple(where))
    return values.at[spots[0]].set(low).at[spots[1]].set(high)


def block_scale(rng, dims, pieces, smallest, top_value):
    loudness = 1.0
    for position, shards_of in pieces:
        steps = jax.random.uniform(jax.random.fold_in(jax.random.fold_in(rng, 6), position), (shards_of,), jnp.float32, smallest / len(pieces), top_value / len(pieces))
        loudness = loudness * jnp.repeat(jnp.exp(steps), dims[position] // shards_of).reshape((-1,) + (1,) * (len(dims) - 1 - position))
    return loudness


def gaussian(stream_key, shape, deviation, bound, split=(), kind=jnp.bfloat16):
    drawn = jax.random.normal(stream_key, shape, jnp.float32) * deviation
    if len(split) > 0:
        drawn = block_scale(stream_key, shape, split, -0.22, 0.18) * drawn
    return jnp.clip(drawn, min=-bound, max=bound).astype(kind)


def setup_inputs(seed: int = 0, part: int = 0) -> dict:
    streams_of = jax.random.split(jax.random.key(seed), 7)
    part_keys = jax.random.split(jax.random.fold_in(streams_of[6], part), 7)
    return {
        "features": gaussian(part_keys[0], (TOKENS, D), 1.0, 6.0, ((0, 128),)),
        "norm_gain": jnp.clip(1.0 + 0.18 * jax.random.normal(streams_of[1], (D,), jnp.float32), 0.1, 1.9),
        "pred_weight": gaussian(streams_of[2], (D, PIX), D ** -0.5, 0.15625),
        "target": gaussian(part_keys[3], (TOKENS, PIX), 1.0, 6.0, ((0, 128),)),
        "patch_mask": touch_ends((jax.random.randint(part_keys[4], (TOKENS,), 0, 4) < 3).astype(jnp.int32), jax.random.fold_in(part_keys[4], 1), 0, 1),
        "band_level": touch_ends(jax.random.randint(streams_of[5], (NBIN,), 1, 17), jax.random.fold_in(streams_of[5], 1), 1, 16).astype(jnp.int32),
    }


def band_weights(band_level, length_y, length_x):
    row_index = jnp.arange(length_y, dtype=jnp.int32)
    col_index = jnp.arange(length_x, dtype=jnp.int32)
    fold_y = jnp.where(row_index < length_y // 2, row_index, length_y - row_index)
    fold_x = jnp.where(col_index < length_x // 2, col_index, length_x - col_index)
    band_y = fold_y * NBIN // (length_y // 2)
    band_x = fold_x * NBIN // (length_x // 2)
    band_index = jnp.minimum(jnp.maximum(band_y[:, None], band_x[None, :]), NBIN - 1)
    return band_level.astype(jnp.float32)[band_index] / 8.0

def reference(features, norm_gain, pred_weight, target, patch_mask, band_level):
    values = features.astype(jnp.float32)
    centre = values - lax.optimization_barrier(jnp.mean(values, axis=-1, keepdims=True))
    spread = lax.optimization_barrier(jnp.mean(centre * centre, axis=-1, keepdims=True))
    normed = (centre * lax.rsqrt(spread + 1e-06) * norm_gain.astype(jnp.float32)).astype(jnp.bfloat16)
    pred = jnp.dot(normed, pred_weight, preferred_element_type=jnp.float32)
    keep = patch_mask.astype(jnp.float32)[:, None]
    error = (pred - target.astype(jnp.float32)) * keep
    image = error.reshape(H // PATCH, PC, PATCH, PATCH, CH).transpose(4, 0, 2, 1, 3).reshape(CH, H, W)
    weights = band_weights(band_level, H, W)
    total = jnp.zeros((), jnp.float32)
    grads = []
    for channel in range(CH):
        spectrum = jnp.fft.fft2(image[channel])
        power = spectrum.real * spectrum.real + spectrum.imag * spectrum.imag
        total = total + jnp.sum(weights * power)
        inverse = jnp.fft.ifft2(weights * spectrum)
        grads.append(2.0 * inverse.real)
    grad_image = jnp.stack(grads)
    loss = total / (H * W) / (CH * H * W)
    pixel_grad = grad_image.reshape(CH, H // PATCH, PATCH, PC, PATCH).transpose(1, 3, 2, 4, 0).reshape(TOKENS, PIX) * keep
    return (pixel_grad, loss.reshape(1))
```

```python
import math

import jax
import jax.numpy as jnp
import numpy as np
import ml_dtypes
from jax import lax
from jax.experimental import pallas as pl
from jax.experimental.pallas import tpu as pltpu
from jax.sharding import PartitionSpec as P

D = 1280
PIX = 1024
TOK = 256
NBIN = 16
N = 128
ZR = 16
QR = 8
MESH = pl.DeviceIdType.MESH
F32 = jnp.float32
BF16 = jnp.bfloat16


def halves(table):
    high = table.astype(ml_dtypes.bfloat16)
    low = (table - high.astype(np.float64)).astype(ml_dtypes.bfloat16)
    return high, low


def lane_of(channel, k2, part):
    return (channel % 2) * 64 + k2 * 4 + (channel // 2) * 2 + part


def token_table():
    t = np.arange(TOK)
    k = np.arange(128)
    angle = 2 * np.pi * np.outer(k, t) / TOK
    top = np.cos(angle) * math.sqrt(2 / TOK)
    low = np.sin(angle) * math.sqrt(2 / TOK)
    top[0] = 1 / math.sqrt(TOK)
    low[0] = (1 - 2 * (t % 2)) / math.sqrt(TOK)
    return np.concatenate([top, low])


def pixel_tables():
    plain = np.zeros((256, 256))
    first = np.zeros((256, 256))
    for pair in range(2):
        for x in range(16):
            for c in range(4):
                a = pair * 64 + x * 4 + c
                b = 128 + a
                for k2 in range(16):
                    re = pair * 128 + lane_of(c, k2, 0)
                    im = pair * 128 + lane_of(c, k2, 1)
                    phi = 2 * math.pi * x * k2 / 16
                    plain[a, re] = math.cos(phi) / 4
                    plain[a, im] = math.sin(phi) / 4
                    plain[b, re] = -math.sin(phi) / 4
                    plain[b, im] = math.cos(phi) / 4
                    if k2 == 0:
                        first[a, re] = 1 / 4
                        first[a, im] = (1 - 2 * (x % 2)) / 4
                    elif k2 < 8:
                        first[a, re] = math.cos(phi) * math.sqrt(2) / 4
                        first[a, im] = math.sin(phi) * math.sqrt(2) / 4
                    else:
                        psi = 2 * math.pi * x * (k2 + 0.5) / 16
                        first[b, re] = math.cos(psi) * math.sqrt(2) / 4
                        first[b, im] = math.sin(psi) * math.sqrt(2) / 4
    return plain, first


def pixel_turn():
    lane = np.arange(128)
    x = (lane % 64) // 4
    angle = 2 * np.pi * np.outer(np.arange(128), x) / 4096
    return np.cos(angle).astype(np.float32), np.sin(angle).astype(np.float32)


def row_tables():
    k = np.arange(128)
    angle = 2 * np.pi * (np.outer(k, k) % 128) / 128
    outer = np.concatenate([np.cos(angle), np.sin(angle)]) / math.sqrt(128)
    s = np.arange(16)
    angle = 2 * np.pi * (np.outer(s, s) % 16) / 16
    eye = np.eye(8)
    inner = np.concatenate([np.kron(np.cos(angle), eye), np.kron(np.sin(angle), eye)]) / 4
    angle = 2 * np.pi * np.outer(s, k) / 2048
    wide = np.broadcast_to(angle[:, :, None], (16, 128, 128))
    return outer, inner, np.cos(wide).astype(np.float32), np.sin(wide).astype(np.float32)


def doubled(table):
    high, low = halves(table)
    return np.concatenate([high, high], axis=1), low


def split(x):
    high = x.astype(BF16)
    return high, (x - high.astype(F32)).astype(BF16)


def mm(a, b, dims=((1,), (0,))):
    return lax.dot_general(a, b, (dims, ((), ())), preferred_element_type=F32)


def times(x, high, low, dims=((1,), (0,))):
    xh, xl = split(x)
    return mm(xh, high, dims) + (mm(xl, high, dims) + mm(xh, low, dims))


def left(high, low, x, dims=((1,), (0,))):
    xh, xl = split(x)
    return mm(high, xh, dims) + (mm(high, xl, dims) + mm(low, xh, dims))


def stacked(double, low, x):
    xh, xl = split(x)
    return mm(double, jnp.concatenate([xh, xl], axis=0)) + mm(low, xh)


def kernel(
    feat, gain, head, targ, mask, level,
    t_hi, t_lo, m_hi, m_lo, s_hi, s_lo, xc, xs, fa_hi, fa_lo, fb_hi, fb_lo, ca, sa,
    out, loss,
    normed, tm_hi, tm_lo, s0, s1, r0, r1, y0, y1, z0, z1, u, wt, part1, part2,
    fsend, frecv, bsend, brecv, lsend, lrecv,
):
    me = lax.axis_index("seq")
    mz = lax.rem(me, ZR)
    mq = me // ZR
    sends, recvs, backs, homes = (s0, s1), (r0, r1), (y0, y1), (z0, z1)

    barrier = pltpu.get_barrier_semaphore()

    @pl.loop(1, N)
    def _(p):
        pl.semaphore_signal(barrier, inc=1, device_id={"seq": lax.rem(me + p, N)}, device_id_type=MESH)

    for row in range(0, TOK, 64):
        values = feat[row : row + 64, :].astype(F32)
        centre = values - jnp.mean(values, axis=-1, keepdims=True)
        spread = jnp.mean(centre * centre, axis=-1, keepdims=True)
        normed[row : row + 64, :] = (centre * lax.rsqrt(spread + 1e-06) * gain[...]).astype(BF16)

    keep = mask[...].astype(F32)
    tm_hi[...] = (t_hi[...].astype(F32) * keep).astype(BF16)
    tm_lo[...] = (t_lo[...].astype(F32) * keep).astype(BF16)

    def scatter(src, dst, send, recv):
        @pl.loop(1, N)
        def _(p):
            t = lax.rem(me + p, N)
            pltpu.make_async_remote_copy(
                src_ref=src.at[pl.ds(pl.multiple_of(t * 8, 8), 8)],
                dst_ref=dst.at[pl.ds(pl.multiple_of(me * 8, 8), 8)],
                send_sem=send,
                recv_sem=recv,
                device_id={"seq": t},
                device_id_type=MESH,
            ).start()

    def await_all(ref, sem):
        whole = ref.at[pl.ds(0, (N - 1) * 8)]
        pltpu.make_async_copy(whole, whole, sem).wait()

    mine = pl.ds(pl.multiple_of(me * 8, 8), 8)

    for h in range(2):
        for g in range(2):
            lo = h * 512 + g * 256
            error = mm(normed[...], head[:, lo : lo + 256]) - targ[:, lo : lo + 256].astype(F32)
            ab = left(tm_hi[...], tm_lo[...], error)
            for pr in range(2):
                r = g * 4 + pr * 2
                a = ab[:128, pr * 128 : pr * 128 + 128]
                b = ab[128:, pr * 128 : pr * 128 + 128]
                a, b = a * xc[...] - b * xs[...], b * xc[...] + a * xs[...]
                both = jnp.concatenate([a, b], axis=1)
                spec = times(both, m_hi[...], m_lo[...])
                first = times(both[:8], s_hi[...], s_lo[...])
                for i in range(2):
                    sends[h][pl.ds(r + i, 128, stride=8), :] = spec[:, i * 128 : i * 128 + 128]
                    sends[h][r + i : r + i + 1, :] = first[:1, i * 128 : i * 128 + 128]
        recvs[h][mine, :] = sends[h][mine, :]
        if h == 0:
            pl.semaphore_wait(barrier, N - 1)
        scatter(sends[h], recvs[h], fsend.at[h], frecv.at[h])

    lane = lax.broadcasted_iota(jnp.int32, (128, 128), 1)
    row = lax.broadcasted_iota(jnp.int32, (128, 128), 0)
    k2 = lax.shift_right_logical(lane, 2) & 15
    band_x = jnp.where(k2 < 8, 2 * k2, 31 - 2 * k2)
    band_x = jnp.where((lane & 1) + k2 * 2 + me * 64 == 1, NBIN - 1, band_x)
    sign = jnp.where(lane < 64, 1.0, -1.0).astype(F32)

    @pl.loop(0, 16)
    def _(jb):
        ky = jb * 8 + (row & 7) + lax.shift_right_logical(row, 3) * 128
        band_y = lax.shift_right_logical(jnp.minimum(ky, 2048 - ky), 6)
        band = jnp.minimum(jnp.maximum(band_y, band_x), NBIN - 1)
        value = jnp.zeros((128, 128), F32)
        for i in range(NBIN):
            value = jnp.where(band == i, level[i].astype(F32), value)
        wt[jb] = value * 0.125

    def swap(x):
        return pltpu.roll(x, 64, 1) * sign[: x.shape[0]]

    for h in range(2):
        await_all(recvs[h], frecv.at[h])
        for r in range(0, 8, 2):
            x = jnp.concatenate([recvs[h][pl.ds(r + i, 128, stride=8), :] for i in range(2)], axis=1)
            pq = stacked(fa_hi[...], fa_lo[...], x)
            for i in range(2):
                p = pq[:128, i * 128 : i * 128 + 128]
                q = pq[128:, i * 128 : i * 128 + 128]
                c, s = ca[h * 8 + r + i], sa[h * 8 + r + i]
                u[h * 8 + r + i] = (c * p - s * q) + swap(c * q + s * p)

    def middle(jb, acc):
        at = [pl.ds(pl.multiple_of(jb * 16 + i * 8, 8), 8) for i in range(2)]
        x = jnp.concatenate([u[:, at[i], :].reshape(128, 128) for i in range(2)], axis=1)
        pq = stacked(fb_hi[...], fb_lo[...], x)
        vs = []
        for i in range(2):
            v = pq[:128, i * 128 : i * 128 + 128] + swap(pq[128:, i * 128 : i * 128 + 128])
            wv = wt[jb * 2 + i] * v
            acc = acc + jnp.sum((wv * v).reshape(16, 8, 128), axis=0)
            vs.append(wv)
        pq = stacked(fb_hi[...], fb_lo[...], jnp.concatenate(vs, axis=1))
        for i in range(2):
            p = pq[:128, i * 128 : i * 128 + 128]
            q = pq[128:, i * 128 : i * 128 + 128]
            c, s = ca[:, at[i], :].reshape(128, 128), sa[:, at[i], :].reshape(128, 128)
            u[:, at[i], :] = ((c * p - s * q) - swap(c * q + s * p)).reshape(16, 8, 128)
        return acc

    acc = lax.fori_loop(0, 8, middle, jnp.zeros((8, 128), F32))

    part1[pl.ds(pl.multiple_of(mz * 8, 8), 8), :] = acc

    @pl.loop(1, ZR)
    def _(p):
        pltpu.make_async_remote_copy(
            src_ref=part1.at[pl.ds(pl.multiple_of(mz * 8, 8), 8)],
            dst_ref=part1.at[pl.ds(pl.multiple_of(mz * 8, 8), 8)],
            send_sem=lsend.at[0],
            recv_sem=lrecv.at[0],
            device_id={"seq": mq * ZR + lax.rem(mz + p, ZR)},
            device_id_type=MESH,
        ).start()

    for h in range(2):
        for r in range(0, 8, 2):
            x = jnp.concatenate([u[h * 8 + r + i] for i in range(2)], axis=1)
            pq = stacked(fa_hi[...], fa_lo[...], x)
            for i in range(2):
                p = pq[:128, i * 128 : i * 128 + 128]
                q = pq[128:, i * 128 : i * 128 + 128]
                backs[h][pl.ds(r + i, 128, stride=8), :] = p - swap(q)
        homes[h][mine, :] = backs[h][mine, :]
        scatter(backs[h], homes[h], bsend.at[h], brecv.at[h])

    near = part1.at[pl.ds(0, (ZR - 1) * 8)]
    pltpu.make_async_copy(near, near, lsend.at[0]).wait()
    pltpu.make_async_copy(near, near, lrecv.at[0]).wait()
    part2[pl.ds(pl.multiple_of(mq * 8, 8), 8), :] = jnp.sum(part1[...].reshape(ZR, 8, 128), axis=0)

    @pl.loop(1, QR)
    def _(p):
        pltpu.make_async_remote_copy(
            src_ref=part2.at[pl.ds(pl.multiple_of(mq * 8, 8), 8)],
            dst_ref=part2.at[pl.ds(pl.multiple_of(mq * 8, 8), 8)],
            send_sem=lsend.at[1],
            recv_sem=lrecv.at[1],
            device_id={"seq": lax.rem(mq + p, QR) * ZR + mz},
            device_id_type=MESH,
        ).start()

    for h in range(2):
        await_all(homes[h], brecv.at[h])
        for g in range(2):
            lo = h * 512 + g * 256
            blocks = []
            for pr in range(2):
                r = g * 4 + pr * 2
                x = jnp.concatenate([homes[h][pl.ds(r + i, 128, stride=8), :] for i in range(2)], axis=1)
                flip = ((1,), (1,))
                spec = times(x, m_hi[...], m_lo[...], flip)
                first = times(x[:8], s_hi[...], s_lo[...], flip)
                top = lax.broadcasted_iota(jnp.int32, (8, 256), 0)
                head8 = jnp.where(top == 0, jnp.broadcast_to(first[:1], (8, 256)), spec[:8])
                spec = jnp.concatenate([head8, spec[8:]], axis=0)
                a, b = spec[:, :128], spec[:, 128:]
                blocks.append(jnp.concatenate([a * xc[...] + b * xs[...], b * xc[...] - a * xs[...]], axis=0))
            grad = left(tm_hi[...], tm_lo[...], jnp.concatenate(blocks, axis=1), ((0,), (0,)))
            out[:, lo : lo + 256] = grad * 2.0

    far = part2.at[pl.ds(0, (QR - 1) * 8)]
    pltpu.make_async_copy(far, far, lsend.at[1]).wait()
    pltpu.make_async_copy(far, far, lrecv.at[1]).wait()
    loss[0] = jnp.sum(part2[...]) * (1.0 / 33554432.0)
    for h in range(2):
        await_all(sends[h], fsend.at[h])
        await_all(backs[h], bsend.at[h])


def shards(features, norm_gain, pred_weight, target, patch_mask, band_level):
    plain, first = pixel_tables()
    outer, inner, ca, sa = row_tables()
    tables = [
        *halves(token_table()), *halves(plain), *halves(first), *pixel_turn(),
        *doubled(outer), *doubled(inner), ca, sa,
    ]
    vmem = pl.BlockSpec(memory_space=pltpu.VMEM)
    smem = pl.BlockSpec(memory_space=pltpu.SMEM)
    dma = pltpu.SemaphoreType.DMA
    block = pltpu.VMEM((N * 8, 128), F32)
    grad, loss = pl.pallas_call(
        kernel,
        out_shape=(jax.ShapeDtypeStruct((TOK, PIX), F32), jax.ShapeDtypeStruct((1,), F32)),
        in_specs=[vmem] * 5 + [smem] + [vmem] * len(tables),
        out_specs=(vmem, smem),
        scratch_shapes=[
            pltpu.VMEM((TOK, D), BF16),
            pltpu.VMEM((TOK, TOK), BF16),
            pltpu.VMEM((TOK, TOK), BF16),
            *[block] * 8,
            pltpu.VMEM((16, 128, 128), F32),
            pltpu.VMEM((16, 128, 128), F32),
            pltpu.VMEM((ZR * 8, 128), F32),
            pltpu.VMEM((QR * 8, 128), F32),
            *[dma((2,))] * 6,
        ],
        compiler_params=pltpu.CompilerParams(
            collective_id=0, has_side_effects=True, vmem_limit_bytes=48 * 2**20
        ),
    )(
        features, norm_gain.reshape(1, D), pred_weight, target, patch_mask.reshape(1, TOK), band_level,
        *[jnp.asarray(table) for table in tables],
    )
    return grad, loss


def solution(mesh):
    in_specs = (
        P(("scene", "seq"), None),
        P(),
        P(),
        P(("scene", "seq"), None),
        P(("scene", "seq")),
        P(),
    )
    out_specs = (P(("scene", "seq"), None), P("scene"))
    return jax.shard_map(shards, mesh=mesh, in_specs=in_specs, out_specs=out_specs, check_vma=False)
```

```python
import math

import jax
import jax.numpy as jnp
import numpy as np
import ml_dtypes
from jax import lax
from jax.experimental import pallas as pl
from jax.experimental.pallas import tpu as pltpu
from jax.sharding import PartitionSpec as P

D = 1280
PIX = 1024
TOK = 256
NBIN = 16
N = 128
ZR = 16
QR = 8
MESH = pl.DeviceIdType.MESH
F32 = jnp.float32
BF16 = jnp.bfloat16


def halves(table):
    high = table.astype(ml_dtypes.bfloat16)
    low = (table - high.astype(np.float64)).astype(ml_dtypes.bfloat16)
    return high, low


def lane_of(channel, k2, part):
    return (channel % 2) * 64 + k2 * 4 + (channel // 2) * 2 + part


def token_table():
    t = np.arange(TOK)
    k = np.arange(128)
    angle = 2 * np.pi * np.outer(k, t) / TOK
    top = np.cos(angle) * math.sqrt(2 / TOK)
    low = np.sin(angle) * math.sqrt(2 / TOK)
    top[0] = 1 / math.sqrt(TOK)
    low[0] = (1 - 2 * (t % 2)) / math.sqrt(TOK)
    return np.concatenate([top, low])


def pixel_tables():
    plain = np.zeros((256, 256))
    first = np.zeros((256, 256))
    for pair in range(2):
        for x in range(16):
            for c in range(4):
                a = pair * 64 + x * 4 + c
                b = 128 + a
                for k2 in range(16):
                    re = pair * 128 + lane_of(c, k2, 0)
                    im = pair * 128 + lane_of(c, k2, 1)
                    phi = 2 * math.pi * x * k2 / 16
                    plain[a, re] = math.cos(phi) / 4
                    plain[a, im] = math.sin(phi) / 4
                    plain[b, re] = -math.sin(phi) / 4
                    plain[b, im] = math.cos(phi) / 4
                    if k2 == 0:
                        first[a, re] = 1 / 4
                        first[a, im] = (1 - 2 * (x % 2)) / 4
                    elif k2 < 8:
                        first[a, re] = math.cos(phi) * math.sqrt(2) / 4
                        first[a, im] = math.sin(phi) * math.sqrt(2) / 4
                    else:
                        psi = 2 * math.pi * x * (k2 + 0.5) / 16
                        first[b, re] = math.cos(psi) * math.sqrt(2) / 4
                        first[b, im] = math.sin(psi) * math.sqrt(2) / 4
    return plain, first


def pixel_turn():
    lane = np.arange(128)
    x = (lane % 64) // 4
    angle = 2 * np.pi * np.outer(np.arange(128), x) / 4096
    return np.cos(angle).astype(np.float32), np.sin(angle).astype(np.float32)


def row_tables():
    k = np.arange(128)
    angle = 2 * np.pi * (np.outer(k, k) % 128) / 128
    outer = np.concatenate([np.cos(angle), np.sin(angle)]) / math.sqrt(128)
    s = np.arange(16)
    angle = 2 * np.pi * (np.outer(s, s) % 16) / 16
    eye = np.eye(8)
    inner = np.concatenate([np.kron(np.cos(angle), eye), np.kron(np.sin(angle), eye)]) / 4
    angle = 2 * np.pi * np.outer(s, k) / 2048
    wide = np.broadcast_to(angle[:, :, None], (16, 128, 128))
    return outer, inner, np.cos(wide).astype(np.float32), np.sin(wide).astype(np.float32)


def doubled(table):
    high, low = halves(table)
    return np.concatenate([high, high], axis=1), low


def split(x):
    high = x.astype(BF16)
    return high, (x - high.astype(F32)).astype(BF16)


def mm(a, b, dims=((1,), (0,))):
    return lax.dot_general(a, b, (dims, ((), ())), preferred_element_type=F32)


def times(x, high, low, dims=((1,), (0,))):
    xh, xl = split(x)
    return mm(xh, high, dims) + (mm(xl, high, dims) + mm(xh, low, dims))


def left(high, low, x, dims=((1,), (0,))):
    xh, xl = split(x)
    return mm(high, xh, dims) + (mm(high, xl, dims) + mm(low, xh, dims))


def stacked(double, low, x):
    xh, xl = split(x)
    return mm(double, jnp.concatenate([xh, xl], axis=0)) + mm(low, xh)


def kernel(
    feat_h, gain_h, head_h, targ_h, mask_h, level_h, mats_h, turn_h, twist_h,
    out, loss,
    feat, gain, head, targ, mask, level, mats, turn, twist,
    normed, tm_hi, tm_lo, s0, s1, r0, r1, y0, y1, z0, z1, u, wt, part1, part2,
    load, go, fsend, frecv, bsend, brecv, lsend, lrecv,
):
    pairs = (
        (feat_h, feat), (gain_h, gain), (mask_h, mask), (mats_h, mats), (head_h, head),
        (targ_h, targ), (turn_h, turn), (level_h, level), (twist_h, twist),
    )
    loads = [pltpu.make_async_copy(src, dst, load.at[i]) for i, (src, dst) in enumerate(pairs)]
    for copy in loads:
        copy.start()
    t_hi, t_lo, m_hi, m_lo, s_hi, s_lo, fa_hi, fb_hi = [mats.at[i] for i in range(8)]
    fa_lo, fb_lo = mats.at[8, :, pl.ds(0, 128)], mats.at[8, :, pl.ds(128, 128)]
    xc, xs, ca, sa = turn.at[0], turn.at[1], twist.at[0], twist.at[1]
    me = lax.axis_index("seq")
    mz = lax.rem(me, ZR)
    mq = me // ZR
    scene = lax.axis_index("scene")
    late = lax.rem(scene, 2) == 1
    twin = {"seq": me, "scene": scene + 1 - 2 * lax.rem(scene, 2)}
    sends, recvs, backs, homes = (s0, s1), (r0, r1), (y0, y1), (z0, z1)

    barrier = pltpu.get_barrier_semaphore()

    @pl.loop(1, N)
    def _(p):
        pl.semaphore_signal(barrier, inc=1, device_id={"seq": lax.rem(me + p, N)}, device_id_type=MESH)

    pl.semaphore_signal(barrier, inc=1, device_id=twin, device_id_type=MESH)
    loads[0].wait()
    loads[1].wait()
    weight = gain[...].reshape(1, D)
    for row in range(0, TOK, 64):
        values = feat[row : row + 64, :].astype(F32)
        centre = values - jnp.mean(values, axis=-1, keepdims=True)
        spread = jnp.mean(centre * centre, axis=-1, keepdims=True)
        normed[row : row + 64, :] = (centre * lax.rsqrt(spread + 1e-06) * weight).astype(BF16)

    loads[2].wait()
    loads[3].wait()
    keep = mask[...].astype(F32)
    tm_hi[...] = (t_hi[...].astype(F32) * keep).astype(BF16)
    tm_lo[...] = (t_lo[...].astype(F32) * keep).astype(BF16)

    def scatter(src, dst, send, recv):
        @pl.loop(1, N)
        def _(p):
            t = lax.rem(me + p, N)
            pltpu.make_async_remote_copy(
                src_ref=src.at[pl.ds(pl.multiple_of(t * 8, 8), 8)],
                dst_ref=dst.at[pl.ds(pl.multiple_of(me * 8, 8), 8)],
                send_sem=send,
                recv_sem=recv,
                device_id={"seq": t},
                device_id_type=MESH,
            ).start()

    def await_all(ref, sem):
        whole = ref.at[pl.ds(0, (N - 1) * 8)]
        pltpu.make_async_copy(whole, whole, sem).wait()

    mine = pl.ds(pl.multiple_of(me * 8, 8), 8)

    for i in (4, 5, 6):
        loads[i].wait()
    for h in range(2):
        for g in range(2):
            lo = h * 512 + g * 256
            error = mm(normed[...], head[:, lo : lo + 256]) - targ[:, lo : lo + 256].astype(F32)
            ab = left(tm_hi[...], tm_lo[...], error)
            for pr in range(2):
                r = g * 4 + pr * 2
                a = ab[:128, pr * 128 : pr * 128 + 128]
                b = ab[128:, pr * 128 : pr * 128 + 128]
                a, b = a * xc[...] - b * xs[...], b * xc[...] + a * xs[...]
                both = jnp.concatenate([a, b], axis=1)
                spec = times(both, m_hi[...], m_lo[...])
                first = times(both[:8], s_hi[...], s_lo[...])
                for i in range(2):
                    sends[h][pl.ds(r + i, 128, stride=8), :] = spec[:, i * 128 : i * 128 + 128]
                    sends[h][r + i : r + i + 1, :] = first[:1, i * 128 : i * 128 + 128]
        recvs[h][mine, :] = sends[h][mine, :]
        if h == 0:
            pl.semaphore_wait(barrier, N)

            @pl.when(late)
            def _():
                pl.semaphore_wait(go, 1)

        scatter(sends[h], recvs[h], fsend.at[h], frecv.at[h])

    loads[7].wait()
    loads[8].wait()
    lane = lax.broadcasted_iota(jnp.int32, (128, 128), 1)
    row = lax.broadcasted_iota(jnp.int32, (128, 128), 0)
    k2 = lax.shift_right_logical(lane, 2) & 15
    band_x = jnp.where(k2 < 8, 2 * k2, 31 - 2 * k2)
    band_x = jnp.where((lane & 1) + k2 * 2 + me * 64 == 1, NBIN - 1, band_x)
    sign = jnp.where(lane < 64, 1.0, -1.0).astype(F32)

    @pl.loop(0, 16)
    def _(jb):
        ky = jb * 8 + (row & 7) + lax.shift_right_logical(row, 3) * 128
        band_y = lax.shift_right_logical(jnp.minimum(ky, 2048 - ky), 6)
        band = jnp.minimum(jnp.maximum(band_y, band_x), NBIN - 1)
        value = jnp.zeros((128, 128), F32)
        for i in range(NBIN):
            value = jnp.where(band == i, level[i].astype(F32), value)
        wt[jb] = value * 0.125

    for h in range(2):
        await_all(sends[h], fsend.at[h])

    @pl.when(jnp.logical_not(late))
    def _():
        pl.semaphore_signal(go, inc=1, device_id=twin, device_id_type=MESH)

    def swap(x):
        return pltpu.roll(x, 64, 1) * sign[: x.shape[0]]

    for h in range(2):
        await_all(recvs[h], frecv.at[h])
        for r in range(0, 8, 2):
            x = jnp.concatenate([recvs[h][pl.ds(r + i, 128, stride=8), :] for i in range(2)], axis=1)
            pq = stacked(fa_hi[...], fa_lo[...], x)
            for i in range(2):
                p = pq[:128, i * 128 : i * 128 + 128]
                q = pq[128:, i * 128 : i * 128 + 128]
                c, s = ca[h * 8 + r + i], sa[h * 8 + r + i]
                u[h * 8 + r + i] = (c * p - s * q) + swap(c * q + s * p)

    def middle(jb, acc):
        at = [pl.ds(pl.multiple_of(jb * 16 + i * 8, 8), 8) for i in range(2)]
        x = jnp.concatenate([u[:, at[i], :].reshape(128, 128) for i in range(2)], axis=1)
        pq = stacked(fb_hi[...], fb_lo[...], x)
        vs = []
        for i in range(2):
            v = pq[:128, i * 128 : i * 128 + 128] + swap(pq[128:, i * 128 : i * 128 + 128])
            wv = wt[jb * 2 + i] * v
            acc = acc + jnp.sum((wv * v).reshape(16, 8, 128), axis=0)
            vs.append(wv)
        pq = stacked(fb_hi[...], fb_lo[...], jnp.concatenate(vs, axis=1))
        for i in range(2):
            p = pq[:128, i * 128 : i * 128 + 128]
            q = pq[128:, i * 128 : i * 128 + 128]
            c, s = ca[:, at[i], :].reshape(128, 128), sa[:, at[i], :].reshape(128, 128)
            u[:, at[i], :] = ((c * p - s * q) - swap(c * q + s * p)).reshape(16, 8, 128)
        return acc

    acc = lax.fori_loop(0, 8, middle, jnp.zeros((8, 128), F32))

    part1[pl.ds(pl.multiple_of(mz * 8, 8), 8), :] = acc

    @pl.loop(1, ZR)
    def _(p):
        pltpu.make_async_remote_copy(
            src_ref=part1.at[pl.ds(pl.multiple_of(mz * 8, 8), 8)],
            dst_ref=part1.at[pl.ds(pl.multiple_of(mz * 8, 8), 8)],
            send_sem=lsend.at[0],
            recv_sem=lrecv.at[0],
            device_id={"seq": mq * ZR + lax.rem(mz + p, ZR)},
            device_id_type=MESH,
        ).start()

    for h in range(2):
        for r in range(0, 8, 2):
            x = jnp.concatenate([u[h * 8 + r + i] for i in range(2)], axis=1)
            pq = stacked(fa_hi[...], fa_lo[...], x)
            for i in range(2):
                p = pq[:128, i * 128 : i * 128 + 128]
                q = pq[128:, i * 128 : i * 128 + 128]
                backs[h][pl.ds(r + i, 128, stride=8), :] = p - swap(q)
        homes[h][mine, :] = backs[h][mine, :]
        scatter(backs[h], homes[h], bsend.at[h], brecv.at[h])

    near = part1.at[pl.ds(0, (ZR - 1) * 8)]
    pltpu.make_async_copy(near, near, lsend.at[0]).wait()
    pltpu.make_async_copy(near, near, lrecv.at[0]).wait()
    part2[pl.ds(pl.multiple_of(mq * 8, 8), 8), :] = jnp.sum(part1[...].reshape(ZR, 8, 128), axis=0)

    @pl.loop(1, QR)
    def _(p):
        pltpu.make_async_remote_copy(
            src_ref=part2.at[pl.ds(pl.multiple_of(mq * 8, 8), 8)],
            dst_ref=part2.at[pl.ds(pl.multiple_of(mq * 8, 8), 8)],
            send_sem=lsend.at[1],
            recv_sem=lrecv.at[1],
            device_id={"seq": lax.rem(mq + p, QR) * ZR + mz},
            device_id_type=MESH,
        ).start()

    for h in range(2):
        await_all(homes[h], brecv.at[h])
        for g in range(2):
            lo = h * 512 + g * 256
            blocks = []
            for pr in range(2):
                r = g * 4 + pr * 2
                x = jnp.concatenate([homes[h][pl.ds(r + i, 128, stride=8), :] for i in range(2)], axis=1)
                flip = ((1,), (1,))
                spec = times(x, m_hi[...], m_lo[...], flip)
                first = times(x[:8], s_hi[...], s_lo[...], flip)
                top = lax.broadcasted_iota(jnp.int32, (8, 256), 0)
                head8 = jnp.where(top == 0, jnp.broadcast_to(first[:1], (8, 256)), spec[:8])
                spec = jnp.concatenate([head8, spec[8:]], axis=0)
                a, b = spec[:, :128], spec[:, 128:]
                blocks.append(jnp.concatenate([a * xc[...] + b * xs[...], b * xc[...] - a * xs[...]], axis=0))
            grad = left(tm_hi[...], tm_lo[...], jnp.concatenate(blocks, axis=1), ((0,), (0,)))
            out[:, lo : lo + 256] = grad * 2.0

    far = part2.at[pl.ds(0, (QR - 1) * 8)]
    pltpu.make_async_copy(far, far, lsend.at[1]).wait()
    pltpu.make_async_copy(far, far, lrecv.at[1]).wait()
    loss[0] = jnp.sum(part2[...]) * (1.0 / 33554432.0)
    for h in range(2):
        await_all(backs[h], bsend.at[h])


def shards(features, norm_gain, pred_weight, target, patch_mask, band_level):
    plain, first = pixel_tables()
    outer, inner, ca, sa = row_tables()
    outer_hi, outer_lo = doubled(outer)
    inner_hi, inner_lo = doubled(inner)
    mats = np.stack([
        *halves(token_table()), *halves(plain), *halves(first), outer_hi, inner_hi,
        np.concatenate([outer_lo, inner_lo], axis=1),
    ])
    tables = [mats, np.stack(pixel_turn()), np.stack([ca, sa])]
    hbm = pl.BlockSpec(memory_space=pltpu.HBM)
    dma = pltpu.SemaphoreType.DMA
    block = pltpu.VMEM((N * 8, 128), F32)
    grad, loss = pl.pallas_call(
        kernel,
        out_shape=(jax.ShapeDtypeStruct((TOK, PIX), F32), jax.ShapeDtypeStruct((1,), F32)),
        in_specs=[hbm] * (6 + len(tables)),
        out_specs=(pl.BlockSpec(memory_space=pltpu.VMEM), pl.BlockSpec(memory_space=pltpu.SMEM)),
        scratch_shapes=[
            pltpu.VMEM((TOK, D), BF16),
            pltpu.VMEM((D,), F32),
            pltpu.VMEM((D, PIX), BF16),
            pltpu.VMEM((TOK, PIX), BF16),
            pltpu.VMEM((1, TOK), jnp.int32),
            pltpu.SMEM((NBIN,), jnp.int32),
            pltpu.VMEM((9, 256, 256), BF16),
            pltpu.VMEM((2, 128, 128), F32),
            pltpu.VMEM((2, 16, 128, 128), F32),
            pltpu.VMEM((TOK, D), BF16),
            pltpu.VMEM((TOK, TOK), BF16),
            pltpu.VMEM((TOK, TOK), BF16),
            *[block] * 8,
            pltpu.VMEM((16, 128, 128), F32),
            pltpu.VMEM((16, 128, 128), F32),
            pltpu.VMEM((ZR * 8, 128), F32),
            pltpu.VMEM((QR * 8, 128), F32),
            dma((9,)),
            pltpu.SemaphoreType.REGULAR,
            *[dma((2,))] * 6,
        ],
        compiler_params=pltpu.CompilerParams(
            collective_id=0, has_side_effects=True, vmem_limit_bytes=32 * 2**20
        ),
    )(
        features, norm_gain, pred_weight, target, patch_mask.reshape(1, TOK), band_level,
        *[jnp.asarray(table) for table in tables],
    )
    return grad, loss


def solution(mesh):
    in_specs = (
        P(("scene", "seq"), None),
        P(),
        P(),
        P(("scene", "seq"), None),
        P(("scene", "seq")),
        P(),
    )
    out_specs = (P(("scene", "seq"), None), P("scene"))
    return jax.shard_map(shards, mesh=mesh, in_specs=in_specs, out_specs=out_specs, check_vma=False)
```

```python
import math

import jax
import jax.numpy as jnp
import numpy as np
import ml_dtypes
from jax import lax
from jax.experimental import pallas as pl
from jax.experimental.pallas import tpu as pltpu
from jax.sharding import PartitionSpec as P

D = 1280
PIX = 1024
TOK = 256
NBIN = 16
N = 128
ZR = 16
QR = 8
MESH = pl.DeviceIdType.MESH
F32 = jnp.float32
BF16 = jnp.bfloat16


def halves(table):
    high = table.astype(ml_dtypes.bfloat16)
    low = (table - high.astype(np.float64)).astype(ml_dtypes.bfloat16)
    return high, low


def lane_of(channel, k2, part):
    return (channel % 2) * 64 + k2 * 4 + (channel // 2) * 2 + part


def token_table():
    t = np.arange(TOK)
    k = np.arange(128)
    angle = 2 * np.pi * np.outer(k, t) / TOK
    top = np.cos(angle) * math.sqrt(2 / TOK)
    low = np.sin(angle) * math.sqrt(2 / TOK)
    top[0] = 1 / math.sqrt(TOK)
    low[0] = (1 - 2 * (t % 2)) / math.sqrt(TOK)
    return np.concatenate([top, low])


def pixel_tables():
    plain = np.zeros((256, 256))
    first = np.zeros((256, 256))
    for pair in range(2):
        for x in range(16):
            for c in range(4):
                a = pair * 64 + x * 4 + c
                b = 128 + a
                for k2 in range(16):
                    re = pair * 128 + lane_of(c, k2, 0)
                    im = pair * 128 + lane_of(c, k2, 1)
                    phi = 2 * math.pi * x * k2 / 16
                    plain[a, re] = math.cos(phi) / 4
                    plain[a, im] = math.sin(phi) / 4
                    plain[b, re] = -math.sin(phi) / 4
                    plain[b, im] = math.cos(phi) / 4
                    if k2 == 0:
                        first[a, re] = 1 / 4
                        first[a, im] = (1 - 2 * (x % 2)) / 4
                    elif k2 < 8:
                        first[a, re] = math.cos(phi) * math.sqrt(2) / 4
                        first[a, im] = math.sin(phi) * math.sqrt(2) / 4
                    else:
                        psi = 2 * math.pi * x * (k2 + 0.5) / 16
                        first[b, re] = math.cos(psi) * math.sqrt(2) / 4
                        first[b, im] = math.sin(psi) * math.sqrt(2) / 4
    return plain, first


def pixel_turn():
    lane = np.arange(128)
    x = (lane % 64) // 4
    angle = 2 * np.pi * np.outer(np.arange(128), x) / 4096
    return np.cos(angle).astype(np.float32), np.sin(angle).astype(np.float32)


def row_tables():
    k = np.arange(128)
    angle = 2 * np.pi * (np.outer(k, k) % 128) / 128
    outer = np.concatenate([np.cos(angle), np.sin(angle)]) / math.sqrt(128)
    s = np.arange(16)
    angle = 2 * np.pi * (np.outer(s, s) % 16) / 16
    eye = np.eye(8)
    inner = np.concatenate([np.kron(np.cos(angle), eye), np.kron(np.sin(angle), eye)]) / 4
    angle = 2 * np.pi * np.outer(s, k) / 2048
    wide = np.broadcast_to(angle[:, :, None], (16, 128, 128))
    return outer, inner, np.cos(wide).astype(np.float32), np.sin(wide).astype(np.float32)


def doubled(table):
    high, low = halves(table)
    return np.concatenate([high, high], axis=1), low


def split(x):
    high = x.astype(BF16)
    return high, (x - high.astype(F32)).astype(BF16)


def mm(a, b, dims=((1,), (0,))):
    return lax.dot_general(a, b, (dims, ((), ())), preferred_element_type=F32)


def times(x, high, low, dims=((1,), (0,))):
    xh, xl = split(x)
    return mm(xh, high, dims) + (mm(xl, high, dims) + mm(xh, low, dims))


def left(high, low, x, dims=((1,), (0,))):
    xh, xl = split(x)
    return mm(high, xh, dims) + (mm(high, xl, dims) + mm(low, xh, dims))


def stacked(double, low, x):
    xh, xl = split(x)
    return mm(double, jnp.concatenate([xh, xl], axis=0)) + mm(low, xh)


def kernel(
    feat_h, gain_h, head_h, targ_h, mask_h, level_h, mats_h, turn_h, twist_h,
    out_h, loss,
    feat, gain, head, targ, mask, level, mats, turn, twist,
    normed, tm_hi, tm_lo, s0, s1, r0, r1, y0, y1, z0, z1, u, wt, part1, part2, out,
    load, save, go, fsend, frecv, bsend, brecv, lsend, lrecv,
):
    pairs = (
        (feat_h, feat), (gain_h, gain), (mask_h, mask), (mats_h, mats), (head_h, head),
        (targ_h, targ), (turn_h, turn), (level_h, level), (twist_h, twist),
    )
    loads = [pltpu.make_async_copy(src, dst, load.at[i]) for i, (src, dst) in enumerate(pairs)]
    for copy in loads:
        copy.start()
    t_hi, t_lo, m_hi, m_lo, s_hi, s_lo, fa_hi, fb_hi = [mats.at[i] for i in range(8)]
    fa_lo, fb_lo = mats.at[8, :, pl.ds(0, 128)], mats.at[8, :, pl.ds(128, 128)]
    xc, xs, ca, sa = turn.at[0], turn.at[1], twist.at[0], twist.at[1]
    me = lax.axis_index("seq")
    mz = lax.rem(me, ZR)
    mq = me // ZR
    scene = lax.axis_index("scene")
    late = lax.rem(scene, 2) == 1
    twin = {"seq": me, "scene": scene + 1 - 2 * lax.rem(scene, 2)}
    sends, recvs, backs, homes = (s0, s1), (r0, r1), (y0, y1), (z0, z1)

    barrier = pltpu.get_barrier_semaphore()

    @pl.loop(1, N)
    def _(p):
        pl.semaphore_signal(barrier, inc=1, device_id={"seq": lax.rem(me + p, N)}, device_id_type=MESH)

    pl.semaphore_signal(barrier, inc=1, device_id=twin, device_id_type=MESH)
    loads[0].wait()
    loads[1].wait()
    weight = gain[...].reshape(1, D)
    for row in range(0, TOK, 64):
        values = feat[row : row + 64, :].astype(F32)
        centre = values - jnp.mean(values, axis=-1, keepdims=True)
        spread = jnp.mean(centre * centre, axis=-1, keepdims=True)
        normed[row : row + 64, :] = (centre * lax.rsqrt(spread + 1e-06) * weight).astype(BF16)

    loads[2].wait()
    loads[3].wait()
    keep = mask[...].astype(F32)
    tm_hi[...] = (t_hi[...].astype(F32) * keep).astype(BF16)
    tm_lo[...] = (t_lo[...].astype(F32) * keep).astype(BF16)

    def scatter(src, dst, send, recv):
        @pl.loop(1, N)
        def _(p):
            t = lax.rem(me + p, N)
            pltpu.make_async_remote_copy(
                src_ref=src.at[pl.ds(pl.multiple_of(t * 8, 8), 8)],
                dst_ref=dst.at[pl.ds(pl.multiple_of(me * 8, 8), 8)],
                send_sem=send,
                recv_sem=recv,
                device_id={"seq": t},
                device_id_type=MESH,
            ).start()

    def await_all(ref, sem):
        whole = ref.at[pl.ds(0, (N - 1) * 8)]
        pltpu.make_async_copy(whole, whole, sem).wait()

    mine = pl.ds(pl.multiple_of(me * 8, 8), 8)

    for i in (4, 5, 6):
        loads[i].wait()
    for h in range(2):
        for g in range(2):
            lo = h * 512 + g * 256
            error = mm(normed[...], head[:, lo : lo + 256]) - targ[:, lo : lo + 256].astype(F32)
            ab = left(tm_hi[...], tm_lo[...], error)
            for pr in range(2):
                r = g * 4 + pr * 2
                a = ab[:128, pr * 128 : pr * 128 + 128]
                b = ab[128:, pr * 128 : pr * 128 + 128]
                a, b = a * xc[...] - b * xs[...], b * xc[...] + a * xs[...]
                both = jnp.concatenate([a, b], axis=1)
                spec = times(both, m_hi[...], m_lo[...])
                first = times(both[:8], s_hi[...], s_lo[...])
                for i in range(2):
                    sends[h][pl.ds(r + i, 128, stride=8), :] = spec[:, i * 128 : i * 128 + 128]
                    sends[h][r + i : r + i + 1, :] = first[:1, i * 128 : i * 128 + 128]
        recvs[h][mine, :] = sends[h][mine, :]
        if h == 0:
            pl.semaphore_wait(barrier, N)

            @pl.when(late)
            def _():
                pl.semaphore_wait(go, 1)

        scatter(sends[h], recvs[h], fsend.at[h], frecv.at[h])

    loads[7].wait()
    loads[8].wait()
    lane = lax.broadcasted_iota(jnp.int32, (128, 128), 1)
    row = lax.broadcasted_iota(jnp.int32, (128, 128), 0)
    k2 = lax.shift_right_logical(lane, 2) & 15
    band_x = jnp.where(k2 < 8, 2 * k2, 31 - 2 * k2)
    band_x = jnp.where((lane & 1) + k2 * 2 + me * 64 == 1, NBIN - 1, band_x)
    sign = jnp.where(lane < 64, 1.0, -1.0).astype(F32)

    @pl.loop(0, 16)
    def _(jb):
        ky = jb * 8 + (row & 7) + lax.shift_right_logical(row, 3) * 128
        band_y = lax.shift_right_logical(jnp.minimum(ky, 2048 - ky), 6)
        band = jnp.minimum(jnp.maximum(band_y, band_x), NBIN - 1)
        value = jnp.zeros((128, 128), F32)
        for i in range(NBIN):
            value = jnp.where(band == i, level[i].astype(F32), value)
        wt[jb] = value * 0.125

    await_all(sends[0], fsend.at[0])

    @pl.when(jnp.logical_not(late))
    def _():
        pl.semaphore_signal(go, inc=1, device_id=twin, device_id_type=MESH)

    await_all(sends[1], fsend.at[1])

    def swap(x):
        return pltpu.roll(x, 64, 1) * sign[: x.shape[0]]

    for h in range(2):
        await_all(recvs[h], frecv.at[h])
        for r in range(0, 8, 2):
            x = jnp.concatenate([recvs[h][pl.ds(r + i, 128, stride=8), :] for i in range(2)], axis=1)
            pq = stacked(fa_hi[...], fa_lo[...], x)
            for i in range(2):
                p = pq[:128, i * 128 : i * 128 + 128]
                q = pq[128:, i * 128 : i * 128 + 128]
                c, s = ca[h * 8 + r + i], sa[h * 8 + r + i]
                u[h * 8 + r + i] = (c * p - s * q) + swap(c * q + s * p)

    def middle(jb, acc):
        at = [pl.ds(jb * 16 + i * 8, 8) for i in range(2)]
        x = jnp.concatenate([u[:, at[i], :].reshape(128, 128) for i in range(2)], axis=1)
        pq = stacked(fb_hi[...], fb_lo[...], x)
        vs = []
        for i in range(2):
            v = pq[:128, i * 128 : i * 128 + 128] + swap(pq[128:, i * 128 : i * 128 + 128])
            wv = wt[jb * 2 + i] * v
            acc = acc + jnp.sum((wv * v).reshape(16, 8, 128), axis=0)
            vs.append(wv)
        pq = stacked(fb_hi[...], fb_lo[...], jnp.concatenate(vs, axis=1))
        for i in range(2):
            p = pq[:128, i * 128 : i * 128 + 128]
            q = pq[128:, i * 128 : i * 128 + 128]
            c, s = ca[:, at[i], :].reshape(128, 128), sa[:, at[i], :].reshape(128, 128)
            u[:, at[i], :] = ((c * p - s * q) - swap(c * q + s * p)).reshape(16, 8, 128)
        return acc

    acc = jnp.zeros((8, 128), F32)
    for jb in range(8):
        acc = middle(jb, acc)

    part1[pl.ds(pl.multiple_of(mz * 8, 8), 8), :] = acc

    @pl.loop(1, ZR)
    def _(p):
        pltpu.make_async_remote_copy(
            src_ref=part1.at[pl.ds(pl.multiple_of(mz * 8, 8), 8)],
            dst_ref=part1.at[pl.ds(pl.multiple_of(mz * 8, 8), 8)],
            send_sem=lsend.at[0],
            recv_sem=lrecv.at[0],
            device_id={"seq": mq * ZR + lax.rem(mz + p, ZR)},
            device_id_type=MESH,
        ).start()

    for h in range(2):
        for r in range(0, 8, 2):
            x = jnp.concatenate([u[h * 8 + r + i] for i in range(2)], axis=1)
            pq = stacked(fa_hi[...], fa_lo[...], x)
            for i in range(2):
                p = pq[:128, i * 128 : i * 128 + 128]
                q = pq[128:, i * 128 : i * 128 + 128]
                backs[h][pl.ds(r + i, 128, stride=8), :] = p - swap(q)
        homes[h][mine, :] = backs[h][mine, :]
        scatter(backs[h], homes[h], bsend.at[h], brecv.at[h])

    near = part1.at[pl.ds(0, (ZR - 1) * 8)]
    pltpu.make_async_copy(near, near, lsend.at[0]).wait()
    pltpu.make_async_copy(near, near, lrecv.at[0]).wait()
    part2[pl.ds(pl.multiple_of(mq * 8, 8), 8), :] = jnp.sum(part1[...].reshape(ZR, 8, 128), axis=0)

    @pl.loop(1, QR)
    def _(p):
        pltpu.make_async_remote_copy(
            src_ref=part2.at[pl.ds(pl.multiple_of(mq * 8, 8), 8)],
            dst_ref=part2.at[pl.ds(pl.multiple_of(mq * 8, 8), 8)],
            send_sem=lsend.at[1],
            recv_sem=lrecv.at[1],
            device_id={"seq": lax.rem(mq + p, QR) * ZR + mz},
            device_id_type=MESH,
        ).start()

    saves = []
    for h in range(2):
        await_all(homes[h], brecv.at[h])
        for g in range(2):
            lo = h * 512 + g * 256
            blocks = []
            for pr in range(2):
                r = g * 4 + pr * 2
                x = jnp.concatenate([homes[h][pl.ds(r + i, 128, stride=8), :] for i in range(2)], axis=1)
                flip = ((1,), (1,))
                spec = times(x, m_hi[...], m_lo[...], flip)
                first = times(x[:8], s_hi[...], s_lo[...], flip)
                top = lax.broadcasted_iota(jnp.int32, (8, 256), 0)
                head8 = jnp.where(top == 0, jnp.broadcast_to(first[:1], (8, 256)), spec[:8])
                spec = jnp.concatenate([head8, spec[8:]], axis=0)
                a, b = spec[:, :128], spec[:, 128:]
                blocks.append(jnp.concatenate([a * xc[...] + b * xs[...], b * xc[...] - a * xs[...]], axis=0))
            grad = left(tm_hi[...], tm_lo[...], jnp.concatenate(blocks, axis=1), ((0,), (0,)))
            out[:, lo : lo + 256] = grad * 2.0
            saves.append(
                pltpu.make_async_copy(
                    out.at[:, pl.ds(lo, 256)], out_h.at[:, pl.ds(lo, 256)], save.at[h * 2 + g]
                )
            )
            saves[-1].start()

    far = part2.at[pl.ds(0, (QR - 1) * 8)]
    pltpu.make_async_copy(far, far, lsend.at[1]).wait()
    pltpu.make_async_copy(far, far, lrecv.at[1]).wait()
    loss[0] = jnp.sum(part2[...]) * (1.0 / 33554432.0)
    for h in range(2):
        await_all(backs[h], bsend.at[h])
    for copy in saves:
        copy.wait()


def shards(features, norm_gain, pred_weight, target, patch_mask, band_level):
    plain, first = pixel_tables()
    outer, inner, ca, sa = row_tables()
    outer_hi, outer_lo = doubled(outer)
    inner_hi, inner_lo = doubled(inner)
    mats = np.stack([
        *halves(token_table()), *halves(plain), *halves(first), outer_hi, inner_hi,
        np.concatenate([outer_lo, inner_lo], axis=1),
    ])
    tables = [mats, np.stack(pixel_turn()), np.stack([ca, sa])]
    hbm = pl.BlockSpec(memory_space=pltpu.HBM)
    dma = pltpu.SemaphoreType.DMA
    block = pltpu.VMEM((N * 8, 128), F32)
    grad, loss = pl.pallas_call(
        kernel,
        out_shape=(jax.ShapeDtypeStruct((TOK, PIX), F32), jax.ShapeDtypeStruct((1,), F32)),
        in_specs=[hbm] * (6 + len(tables)),
        out_specs=(hbm, pl.BlockSpec(memory_space=pltpu.SMEM)),
        scratch_shapes=[
            pltpu.VMEM((TOK, D), BF16),
            pltpu.VMEM((D,), F32),
            pltpu.VMEM((D, PIX), BF16),
            pltpu.VMEM((TOK, PIX), BF16),
            pltpu.VMEM((1, TOK), jnp.int32),
            pltpu.SMEM((NBIN,), jnp.int32),
            pltpu.VMEM((9, 256, 256), BF16),
            pltpu.VMEM((2, 128, 128), F32),
            pltpu.VMEM((2, 16, 128, 128), F32),
            pltpu.VMEM((TOK, D), BF16),
            pltpu.VMEM((TOK, TOK), BF16),
            pltpu.VMEM((TOK, TOK), BF16),
            *[block] * 8,
            pltpu.VMEM((16, 128, 128), F32),
            pltpu.VMEM((16, 128, 128), F32),
            pltpu.VMEM((ZR * 8, 128), F32),
            pltpu.VMEM((QR * 8, 128), F32),
            pltpu.VMEM((TOK, PIX), F32),
            dma((9,)),
            dma((4,)),
            pltpu.SemaphoreType.REGULAR,
            *[dma((2,))] * 6,
        ],
        compiler_params=pltpu.CompilerParams(
            collective_id=0, has_side_effects=True, vmem_limit_bytes=60 * 2**20
        ),
    )(
        features, norm_gain, pred_weight, target, patch_mask.reshape(1, TOK), band_level,
        *[jnp.asarray(table) for table in tables],
    )
    return grad, loss


def solution(mesh):
    in_specs = (
        P(("scene", "seq"), None),
        P(),
        P(),
        P(("scene", "seq"), None),
        P(("scene", "seq")),
        P(),
    )
    out_specs = (P(("scene", "seq"), None), P("scene"))
    return jax.shard_map(shards, mesh=mesh, in_specs=in_specs, out_specs=out_specs, check_vma=False)
```

```python
import math

import jax
import jax.numpy as jnp
import numpy as np
import ml_dtypes
from jax import lax
from jax.experimental import pallas as pl
from jax.experimental.pallas import tpu as pltpu
from jax.sharding import PartitionSpec as P

D = 1280
PIX = 1024
TOK = 256
NBIN = 16
N = 128
ZR = 16
QR = 8
MESH = pl.DeviceIdType.MESH
F32 = jnp.float32
BF16 = jnp.bfloat16


def halves(table):
    high = table.astype(ml_dtypes.bfloat16)
    low = (table - high.astype(np.float64)).astype(ml_dtypes.bfloat16)
    return high, low


def lane_of(channel, k2, part):
    return (channel % 2) * 64 + k2 * 4 + (channel // 2) * 2 + part


def token_table():
    t = np.arange(TOK)
    k = np.arange(128)
    angle = 2 * np.pi * np.outer(k, t) / TOK
    top = np.cos(angle) * math.sqrt(2 / TOK)
    low = np.sin(angle) * math.sqrt(2 / TOK)
    top[0] = 1 / math.sqrt(TOK)
    low[0] = (1 - 2 * (t % 2)) / math.sqrt(TOK)
    return np.concatenate([top, low])


def pixel_tables():
    plain = np.zeros((256, 256))
    first = np.zeros((256, 256))
    for pair in range(2):
        for x in range(16):
            for c in range(4):
                a = pair * 64 + x * 4 + c
                b = 128 + a
                for k2 in range(16):
                    re = pair * 128 + lane_of(c, k2, 0)
                    im = pair * 128 + lane_of(c, k2, 1)
                    phi = 2 * math.pi * x * k2 / 16
                    plain[a, re] = math.cos(phi) / 4
                    plain[a, im] = math.sin(phi) / 4
                    plain[b, re] = -math.sin(phi) / 4
                    plain[b, im] = math.cos(phi) / 4
                    if k2 == 0:
                        first[a, re] = 1 / 4
                        first[a, im] = (1 - 2 * (x % 2)) / 4
                    elif k2 < 8:
                        first[a, re] = math.cos(phi) * math.sqrt(2) / 4
                        first[a, im] = math.sin(phi) * math.sqrt(2) / 4
                    else:
                        psi = 2 * math.pi * x * (k2 + 0.5) / 16
                        first[b, re] = math.cos(psi) * math.sqrt(2) / 4
                        first[b, im] = math.sin(psi) * math.sqrt(2) / 4
    return plain, first


def pixel_turn():
    lane = np.arange(128)
    x = (lane % 64) // 4
    angle = 2 * np.pi * np.outer(np.arange(128), x) / 4096
    return np.cos(angle).astype(np.float32), np.sin(angle).astype(np.float32)


def row_tables():
    k = np.arange(128)
    angle = 2 * np.pi * (np.outer(k, k) % 128) / 128
    outer = np.concatenate([np.cos(angle), np.sin(angle)]) / math.sqrt(128)
    s = np.arange(16)
    angle = 2 * np.pi * (np.outer(s, s) % 16) / 16
    eye = np.eye(8)
    inner = np.concatenate([np.kron(np.cos(angle), eye), np.kron(np.sin(angle), eye)]) / 4
    angle = 2 * np.pi * np.outer(s, k) / 2048
    wide = np.broadcast_to(angle[:, :, None], (16, 128, 128))
    return outer, inner, np.cos(wide).astype(np.float32), np.sin(wide).astype(np.float32)


def doubled(table):
    high, low = halves(table)
    return np.concatenate([high, high], axis=1), low


def split(x):
    high = x.astype(BF16)
    return high, (x - high.astype(F32)).astype(BF16)


def mm(a, b, dims=((1,), (0,))):
    return lax.dot_general(a, b, (dims, ((), ())), preferred_element_type=F32)


def times(x, high, low, dims=((1,), (0,))):
    xh, xl = split(x)
    return mm(xh, high, dims) + (mm(xl, high, dims) + mm(xh, low, dims))


def left(high, low, x, dims=((1,), (0,))):
    xh, xl = split(x)
    return mm(high, xh, dims) + (mm(high, xl, dims) + mm(low, xh, dims))


def stacked(double, low, x):
    xh, xl = split(x)
    return mm(double, jnp.concatenate([xh, xl], axis=0)) + mm(low, xh)


def kernel(
    feat_h, gain_h, head_h, targ_h, mask_h, level_h, mats_h, turn_h, twist_h,
    out_h, loss,
    feat, gain, head, targ, mask, level, mats, turn, twist,
    normed, tm_hi, tm_lo, s0, s1, r0, r1, y0, y1, z0, z1, u, wt, part1, part2, out, own,
    load, save, go, fsend, frecv, bsend, brecv, lsend, lrecv,
):
    pairs = (
        (feat_h, feat), (gain_h, gain), (mask_h, mask), (mats_h, mats), (head_h, head),
        (targ_h, targ), (turn_h, turn), (level_h, level), (twist_h, twist),
    )
    loads = [pltpu.make_async_copy(src, dst, load.at[i]) for i, (src, dst) in enumerate(pairs)]
    for copy in loads:
        copy.start()
    t_hi, t_lo, m_hi, m_lo, s_hi, s_lo, fa_hi, fb_hi = [mats.at[i] for i in range(8)]
    fa_lo, fb_lo = mats.at[8, :, pl.ds(0, 128)], mats.at[8, :, pl.ds(128, 128)]
    xc, xs, ca, sa = turn.at[0], turn.at[1], twist.at[0], twist.at[1]
    me = lax.axis_index("seq")
    mz = lax.rem(me, ZR)
    mq = me // ZR
    scene = lax.axis_index("scene")
    late = lax.rem(scene, 2) == 1
    twin = {"seq": me, "scene": scene + 1 - 2 * lax.rem(scene, 2)}
    sends, recvs, backs, homes = (s0, s1), (r0, r1), (y0, y1), (z0, z1)

    barrier = pltpu.get_barrier_semaphore()

    @pl.loop(1, N)
    def _(p):
        pl.semaphore_signal(barrier, inc=1, device_id={"seq": lax.rem(me + p, N)}, device_id_type=MESH)

    pl.semaphore_signal(barrier, inc=1, device_id=twin, device_id_type=MESH)
    loads[0].wait()
    loads[1].wait()
    weight = gain[...].reshape(1, D)
    for row in range(0, TOK, 64):
        values = feat[row : row + 64, :].astype(F32)
        centre = values - jnp.mean(values, axis=-1, keepdims=True)
        spread = jnp.mean(centre * centre, axis=-1, keepdims=True)
        normed[row : row + 64, :] = (centre * lax.rsqrt(spread + 1e-06) * weight).astype(BF16)

    loads[2].wait()
    loads[3].wait()
    keep = mask[...].astype(F32)
    tm_hi[...] = (t_hi[...].astype(F32) * keep).astype(BF16)
    tm_lo[...] = (t_lo[...].astype(F32) * keep).astype(BF16)

    def scatter(src, dst, send, recv, rows):
        @pl.loop(1, N)
        def _(p):
            t = lax.rem(me + p, N)
            pltpu.make_async_remote_copy(
                src_ref=src.at[pl.ds(pl.multiple_of(t * 8, 8), rows)],
                dst_ref=dst.at[pl.ds(pl.multiple_of(me * 8, 8), rows)],
                send_sem=send,
                recv_sem=recv,
                device_id={"seq": t},
                device_id_type=MESH,
            ).start()

    def await_all(ref, sem, rows):
        whole = ref.at[pl.ds(0, (N - 1) * rows)]
        pltpu.make_async_copy(whole, whole, sem).wait()

    mine = pl.ds(pl.multiple_of(me * 8, 8), 8)
    lane = lax.broadcasted_iota(jnp.int32, (128, 128), 1)
    row = lax.broadcasted_iota(jnp.int32, (128, 128), 0)
    k2 = lax.shift_right_logical(lane, 2) & 15
    top_band = k2 == 8

    def spare(r, drop):
        group = r - (drop == 0)
        group = group + (group > 7)
        return group, 32 - 4 * group

    def packed(x, dropped, r, drop):
        return jnp.where(top_band, pltpu.roll(dropped, spare(r, drop)[1] % 128, 1), x)

    def unpacked(blocks, drop):
        dropped = jnp.zeros((128, 128), F32)
        for r in range(16):
            if r != drop:
                group, shift = spare(r, drop)
                moved = pltpu.roll(rows_of(blocks, r, drop), -shift % 128, 1)
                dropped = jnp.where(k2 == group, moved, dropped)
        return dropped

    def rows_of(blocks, r, drop):
        return blocks[r // 8][pl.ds(r % 8 - (drop == 0 and r < 8), 128, stride=8), :]

    def put_rows(blocks, r, x, drop):
        blocks[r // 8][pl.ds(r % 8 - (drop == 0 and r < 8), 128, stride=8), :] = x

    def with_first(spec, first):
        top = lax.broadcasted_iota(jnp.int32, (8, 256), 0)
        head8 = jnp.where(top == 0, jnp.broadcast_to(first[:1], (8, 256)), spec[:8])
        return jnp.concatenate([head8, spec[8:]], axis=0)

    for i in (4, 5, 6):
        loads[i].wait()
    for h in range(2):
        for g in range(2):
            lo = h * 512 + g * 256
            error = mm(normed[...], head[:, lo : lo + 256]) - targ[:, lo : lo + 256].astype(F32)
            ab = left(tm_hi[...], tm_lo[...], error)
            for pr in range(2):
                r = h * 8 + g * 4 + pr * 2
                a = ab[:128, pr * 128 : pr * 128 + 128]
                b = ab[128:, pr * 128 : pr * 128 + 128]
                a, b = a * xc[...] - b * xs[...], b * xc[...] + a * xs[...]
                both = jnp.concatenate([a, b], axis=1)
                spec = with_first(times(both, m_hi[...], m_lo[...]), times(both[:8], s_hi[...], s_lo[...]))
                for i in range(2):
                    part = spec[:, i * 128 : i * 128 + 128]
                    own[r + i] = part
                    if r + i == 0:
                        zeroth = part
                    else:
                        put_rows(sends, r + i, packed(part, zeroth, r + i, 0), 0)
        recvs[h][mine, :] = sends[h][mine, :]
        if h == 0:
            pl.semaphore_wait(barrier, N)

            @pl.when(late)
            def _():
                pl.semaphore_wait(go, 1)

        scatter(sends[h], recvs[h], fsend.at[h], frecv.at[h], 7 + h)

    loads[7].wait()
    loads[8].wait()
    band_x = jnp.where(k2 < 8, 2 * k2, 31 - 2 * k2)
    band_x = jnp.where((lane & 1) + k2 * 2 + me * 64 == 1, NBIN - 1, band_x)
    sign = jnp.where(lane < 64, 1.0, -1.0).astype(F32)

    @pl.loop(0, 16)
    def _(jb):
        ky = jb * 8 + (row & 7) + lax.shift_right_logical(row, 3) * 128
        band_y = lax.shift_right_logical(jnp.minimum(ky, 2048 - ky), 6)
        band = jnp.minimum(jnp.maximum(band_y, band_x), NBIN - 1)
        value = jnp.zeros((128, 128), F32)
        for i in range(NBIN):
            value = jnp.where(band == i, level[i].astype(F32), value)
        wt[jb] = jnp.where(top_band, 0.0, value * 0.125)

    level_top = level[NBIN - 1].astype(F32) * 0.125
    acc = jnp.zeros((8, 128), F32)
    for r in range(16):
        part = jnp.where(top_band, own[r], 0.0)
        scaled = level_top * part
        own[r] = scaled
        acc = acc + jnp.sum((scaled * part).reshape(16, 8, 128), axis=0)

    await_all(sends[0], fsend.at[0], 7)

    @pl.when(jnp.logical_not(late))
    def _():
        pl.semaphore_signal(go, inc=1, device_id=twin, device_id_type=MESH)

    await_all(sends[1], fsend.at[1], 8)

    def swap(x):
        return pltpu.roll(x, 64, 1) * sign[: x.shape[0]]

    def outward(r, xs2):
        pq = stacked(fa_hi[...], fa_lo[...], jnp.concatenate(xs2, axis=1))
        for i in range(len(xs2)):
            p = pq[:128, i * 128 : i * 128 + 128]
            q = pq[128:, i * 128 : i * 128 + 128]
            c, s = ca[r + i], sa[r + i]
            u[r + i] = (c * p - s * q) + swap(c * q + s * p)

    await_all(recvs[0], frecv.at[0], 7)
    for r in range(2, 8, 2):
        outward(r, [rows_of(recvs, r, 0), rows_of(recvs, r + 1, 0)])
    await_all(recvs[1], frecv.at[1], 8)
    outward(0, [unpacked(recvs, 0), rows_of(recvs, 1, 0)])
    for r in range(8, 16, 2):
        outward(r, [rows_of(recvs, r, 0), rows_of(recvs, r + 1, 0)])

    def middle(jb, acc):
        at = [pl.ds(jb * 16 + i * 8, 8) for i in range(2)]
        x = jnp.concatenate([u[:, at[i], :].reshape(128, 128) for i in range(2)], axis=1)
        pq = stacked(fb_hi[...], fb_lo[...], x)
        vs = []
        for i in range(2):
            v = pq[:128, i * 128 : i * 128 + 128] + swap(pq[128:, i * 128 : i * 128 + 128])
            wv = wt[jb * 2 + i] * v
            acc = acc + jnp.sum((wv * v).reshape(16, 8, 128), axis=0)
            vs.append(wv)
        pq = stacked(fb_hi[...], fb_lo[...], jnp.concatenate(vs, axis=1))
        for i in range(2):
            p = pq[:128, i * 128 : i * 128 + 128]
            q = pq[128:, i * 128 : i * 128 + 128]
            c, s = ca[:, at[i], :].reshape(128, 128), sa[:, at[i], :].reshape(128, 128)
            u[:, at[i], :] = ((c * p - s * q) - swap(c * q + s * p)).reshape(16, 8, 128)
        return acc

    for jb in range(8):
        acc = middle(jb, acc)

    part1[pl.ds(pl.multiple_of(mz * 8, 8), 8), :] = acc

    @pl.loop(1, ZR)
    def _(p):
        pltpu.make_async_remote_copy(
            src_ref=part1.at[pl.ds(pl.multiple_of(mz * 8, 8), 8)],
            dst_ref=part1.at[pl.ds(pl.multiple_of(mz * 8, 8), 8)],
            send_sem=lsend.at[0],
            recv_sem=lrecv.at[0],
            device_id={"seq": mq * ZR + lax.rem(mz + p, ZR)},
            device_id_type=MESH,
        ).start()

    last = None
    for r in (14, 0, 2, 4, 6, 8, 10, 12):
        pq = stacked(fa_hi[...], fa_lo[...], jnp.concatenate([u[r], u[r + 1]], axis=1))
        columns = []
        for i in range(2):
            p = pq[:128, i * 128 : i * 128 + 128]
            q = pq[128:, i * 128 : i * 128 + 128]
            columns.append(p - swap(q))
        if r == 14:
            last = columns[1]
        for i in range(2):
            if r + i != 15:
                put_rows(backs, r + i, packed(columns[i], last, r + i, 15), 15)
        if r == 6 or r == 12:
            h = r // 8
            homes[h][mine, :] = backs[h][mine, :]
            scatter(backs[h], homes[h], bsend.at[h], brecv.at[h], 8 - h)

    near = part1.at[pl.ds(0, (ZR - 1) * 8)]
    pltpu.make_async_copy(near, near, lsend.at[0]).wait()
    pltpu.make_async_copy(near, near, lrecv.at[0]).wait()
    part2[pl.ds(pl.multiple_of(mq * 8, 8), 8), :] = jnp.sum(part1[...].reshape(ZR, 8, 128), axis=0)

    @pl.loop(1, QR)
    def _(p):
        pltpu.make_async_remote_copy(
            src_ref=part2.at[pl.ds(pl.multiple_of(mq * 8, 8), 8)],
            dst_ref=part2.at[pl.ds(pl.multiple_of(mq * 8, 8), 8)],
            send_sem=lsend.at[1],
            recv_sem=lrecv.at[1],
            device_id={"seq": lax.rem(mq + p, QR) * ZR + mz},
            device_id_type=MESH,
        ).start()

    saves = []

    def home_row(r):
        return jnp.where(top_band, own[r], unpacked(homes, 15) if r == 15 else rows_of(homes, r, 15))

    def inward(g):
        blocks = []
        for pr in range(2):
            r = g * 4 + pr * 2
            x = jnp.concatenate([home_row(r), home_row(r + 1)], axis=1)
            flip = ((1,), (1,))
            spec = with_first(times(x, m_hi[...], m_lo[...], flip), times(x[:8], s_hi[...], s_lo[...], flip))
            a, b = spec[:, :128], spec[:, 128:]
            blocks.append(jnp.concatenate([a * xc[...] + b * xs[...], b * xc[...] - a * xs[...]], axis=0))
        grad = left(tm_hi[...], tm_lo[...], jnp.concatenate(blocks, axis=1), ((0,), (0,)))
        lo = g * 256
        out[:, lo : lo + 256] = grad
        saves.append(
            pltpu.make_async_copy(out.at[:, pl.ds(lo, 256)], out_h.at[:, pl.ds(lo, 256)], save.at[g])
        )
        saves[-1].start()

    for h in range(2):
        await_all(homes[h], brecv.at[h], 8 - h)
        for g in range(2):
            inward(h * 2 + g)

    far = part2.at[pl.ds(0, (QR - 1) * 8)]
    pltpu.make_async_copy(far, far, lsend.at[1]).wait()
    pltpu.make_async_copy(far, far, lrecv.at[1]).wait()
    loss[0] = jnp.sum(part2[...])
    for h in range(2):
        await_all(backs[h], bsend.at[h], 8 - h)
    for copy in saves:
        copy.wait()


def shards(features, norm_gain, pred_weight, target, patch_mask, band_level):
    plain, first = pixel_tables()
    outer, inner, ca, sa = row_tables()
    outer_hi, outer_lo = doubled(outer)
    inner_hi, inner_lo = doubled(inner)
    mats = np.stack([
        *halves(token_table()), *halves(plain), *halves(first), outer_hi, inner_hi,
        np.concatenate([outer_lo, inner_lo], axis=1),
    ])
    tables = [mats, np.stack(pixel_turn()), np.stack([ca, sa])]
    hbm = pl.BlockSpec(memory_space=pltpu.HBM)
    dma = pltpu.SemaphoreType.DMA
    block = pltpu.VMEM((N * 8, 128), F32)
    grad, loss = pl.pallas_call(
        kernel,
        out_shape=(jax.ShapeDtypeStruct((TOK, PIX), F32), jax.ShapeDtypeStruct((1,), F32)),
        in_specs=[hbm] * (6 + len(tables)),
        out_specs=(hbm, pl.BlockSpec(memory_space=pltpu.SMEM)),
        scratch_shapes=[
            pltpu.VMEM((TOK, D), BF16),
            pltpu.VMEM((D,), F32),
            pltpu.VMEM((D, PIX), BF16),
            pltpu.VMEM((TOK, PIX), BF16),
            pltpu.VMEM((1, TOK), jnp.int32),
            pltpu.SMEM((NBIN,), jnp.int32),
            pltpu.VMEM((9, 256, 256), BF16),
            pltpu.VMEM((2, 128, 128), F32),
            pltpu.VMEM((2, 16, 128, 128), F32),
            pltpu.VMEM((TOK, D), BF16),
            pltpu.VMEM((TOK, TOK), BF16),
            pltpu.VMEM((TOK, TOK), BF16),
            *[block] * 8,
            pltpu.VMEM((16, 128, 128), F32),
            pltpu.VMEM((16, 128, 128), F32),
            pltpu.VMEM((ZR * 8, 128), F32),
            pltpu.VMEM((QR * 8, 128), F32),
            pltpu.VMEM((TOK, PIX), F32),
            pltpu.VMEM((16, 128, 128), F32),
            dma((9,)),
            dma((4,)),
            pltpu.SemaphoreType.REGULAR,
            *[dma((2,))] * 6,
        ],
        compiler_params=pltpu.CompilerParams(
            collective_id=0, has_side_effects=True, vmem_limit_bytes=60 * 2**20
        ),
    )(
        features, norm_gain, pred_weight, target, patch_mask.reshape(1, TOK), band_level,
        *[jnp.asarray(table) for table in tables],
    )
    return grad * 2.0, loss * (1.0 / 33554432.0)


def solution(mesh):
    in_specs = (
        P(("scene", "seq"), None),
        P(),
        P(),
        P(("scene", "seq"), None),
        P(("scene", "seq")),
        P(),
    )
    out_specs = (P(("scene", "seq"), None), P("scene"))
    return jax.shard_map(shards, mesh=mesh, in_specs=in_specs, out_specs=out_specs, check_vma=False)
```

```python
import math

import jax
import jax.numpy as jnp
import numpy as np
import ml_dtypes
from jax import lax
from jax.experimental import pallas as pl
from jax.experimental.pallas import tpu as pltpu
from jax.sharding import PartitionSpec as P

D = 1280
PIX = 1024
TOK = 256
NBIN = 16
N = 128
ZR = 16
QR = 8
MESH = pl.DeviceIdType.MESH
F32 = jnp.float32
BF16 = jnp.bfloat16


def halves(table):
    high = table.astype(ml_dtypes.bfloat16)
    low = (table - high.astype(np.float64)).astype(ml_dtypes.bfloat16)
    return high, low


def lane_of(channel, k2, part):
    return (channel % 2) * 64 + k2 * 4 + (channel // 2) * 2 + part


def token_table():
    t = np.arange(TOK)
    k = np.arange(128)
    angle = 2 * np.pi * np.outer(k, t) / TOK
    top = np.cos(angle) * math.sqrt(2 / TOK)
    low = np.sin(angle) * math.sqrt(2 / TOK)
    top[0] = 1 / math.sqrt(TOK)
    low[0] = (1 - 2 * (t % 2)) / math.sqrt(TOK)
    return np.concatenate([top, low])


def pixel_tables():
    plain = np.zeros((256, 256))
    first = np.zeros((256, 256))
    for pair in range(2):
        for x in range(16):
            for c in range(4):
                a = pair * 64 + x * 4 + c
                b = 128 + a
                for k2 in range(16):
                    re = pair * 128 + lane_of(c, k2, 0)
                    im = pair * 128 + lane_of(c, k2, 1)
                    phi = 2 * math.pi * x * k2 / 16
                    plain[a, re] = math.cos(phi) / 4
                    plain[a, im] = math.sin(phi) / 4
                    plain[b, re] = -math.sin(phi) / 4
                    plain[b, im] = math.cos(phi) / 4
                    if k2 == 0:
                        first[a, re] = 1 / 4
                        first[a, im] = (1 - 2 * (x % 2)) / 4
                    elif k2 < 8:
                        first[a, re] = math.cos(phi) * math.sqrt(2) / 4
                        first[a, im] = math.sin(phi) * math.sqrt(2) / 4
                    else:
                        psi = 2 * math.pi * x * (k2 + 0.5) / 16
                        first[b, re] = math.cos(psi) * math.sqrt(2) / 4
                        first[b, im] = math.sin(psi) * math.sqrt(2) / 4
    return plain, first


def pixel_turn():
    lane = np.arange(128)
    x = (lane % 64) // 4
    angle = 2 * np.pi * np.outer(np.arange(128), x) / 4096
    return np.cos(angle).astype(np.float32), np.sin(angle).astype(np.float32)


def row_tables():
    k = np.arange(128)
    angle = 2 * np.pi * (np.outer(k, k) % 128) / 128
    outer = np.concatenate([np.cos(angle), np.sin(angle)]) / math.sqrt(128)
    s = np.arange(16)
    angle = 2 * np.pi * (np.outer(s, s) % 16) / 16
    eye = np.eye(8)
    inner = np.concatenate([np.kron(np.cos(angle), eye), np.kron(np.sin(angle), eye)]) / 4
    angle = 2 * np.pi * np.outer(s, k) / 2048
    wide = np.broadcast_to(angle[:, :, None], (16, 128, 128))
    return outer, inner, np.cos(wide).astype(np.float32), np.sin(wide).astype(np.float32)


def doubled(table):
    high, low = halves(table)
    return np.concatenate([high, high], axis=1), low


def split(x):
    high = x.astype(BF16)
    return high, (x - high.astype(F32)).astype(BF16)


def mm(a, b, dims=((1,), (0,))):
    return lax.dot_general(a, b, (dims, ((), ())), preferred_element_type=F32)


def times(x, high, low, dims=((1,), (0,))):
    xh, xl = split(x)
    return mm(xh, high, dims) + (mm(xl, high, dims) + mm(xh, low, dims))


def left(high, low, x, dims=((1,), (0,))):
    xh, xl = split(x)
    return mm(high, xh, dims) + (mm(high, xl, dims) + mm(low, xh, dims))


def stacked(double, low, x):
    xh, xl = split(x)
    return mm(double, jnp.concatenate([xh, xl], axis=0)) + mm(low, xh)


def kernel(
    feat_h, gain_h, head_h, targ_h, mask_h, level_h, mats_h, turn_h, twist_h,
    out_h, loss,
    feat, gain, head, targ, mask, level, mats, turn, twist,
    normed, tm_hi, tm_lo, s0, s1, r0, r1, y0, y1, z0, z1, u, wt, part1, part2, out, own,
    load, save, go, fsend, frecv, bsend, brecv, lsend, lrecv,
):
    pairs = (
        (feat_h, feat), (gain_h, gain), (mask_h, mask), (mats_h, mats), (head_h, head),
        (targ_h, targ), (turn_h, turn), (level_h, level), (twist_h, twist),
    )
    loads = [pltpu.make_async_copy(src, dst, load.at[i]) for i, (src, dst) in enumerate(pairs)]
    for copy in loads:
        copy.start()
    t_hi, t_lo, m_hi, m_lo, s_hi, s_lo, fa_hi, fb_hi = [mats.at[i] for i in range(8)]
    fa_lo, fb_lo = mats.at[8, :, pl.ds(0, 128)], mats.at[8, :, pl.ds(128, 128)]
    xc, xs, ca, sa = turn.at[0], turn.at[1], twist.at[0], twist.at[1]
    me = lax.axis_index("seq")
    mz = lax.rem(me, ZR)
    mq = me // ZR
    scene = lax.axis_index("scene")
    late = lax.rem(scene, 2) == 1
    twin = {"seq": me, "scene": scene + 1 - 2 * lax.rem(scene, 2)}
    sends, recvs, backs, homes = (s0, s1), (r0, r1), (y0, y1), (z0, z1)

    barrier = pltpu.get_barrier_semaphore()

    @pl.loop(1, N)
    def _(p):
        pl.semaphore_signal(barrier, inc=1, device_id={"seq": lax.rem(me + p, N)}, device_id_type=MESH)

    pl.semaphore_signal(barrier, inc=1, device_id=twin, device_id_type=MESH)
    loads[0].wait()
    loads[1].wait()
    weight = gain[...].reshape(1, D)
    for row in range(0, TOK, 64):
        values = feat[row : row + 64, :].astype(F32)
        centre = values - jnp.mean(values, axis=-1, keepdims=True)
        spread = jnp.mean(centre * centre, axis=-1, keepdims=True)
        normed[row : row + 64, :] = (centre * lax.rsqrt(spread + 1e-06) * weight).astype(BF16)

    loads[2].wait()
    loads[3].wait()
    keep = mask[...].astype(F32)
    tm_hi[...] = (t_hi[...].astype(F32) * keep).astype(BF16)
    tm_lo[...] = (t_lo[...].astype(F32) * keep).astype(BF16)

    def scatter(src, dst, send, recv, rows, by_z=False):
        @pl.loop(1, N)
        def _(p):
            if by_z:
                step = p - 1
                step = step + (step >= mz * QR)
                t = lax.rem(mq + lax.rem(step, QR), QR) * ZR + step // QR
            else:
                t = lax.rem(me + p, N)
            pltpu.make_async_remote_copy(
                src_ref=src.at[pl.ds(pl.multiple_of(t * 8, 8), rows)],
                dst_ref=dst.at[pl.ds(pl.multiple_of(me * 8, 8), rows)],
                send_sem=send,
                recv_sem=recv,
                device_id={"seq": t},
                device_id_type=MESH,
            ).start()

    def await_all(ref, sem, rows):
        whole = ref.at[pl.ds(0, (N - 1) * rows)]
        pltpu.make_async_copy(whole, whole, sem).wait()

    mine = pl.ds(pl.multiple_of(me * 8, 8), 8)
    lane = lax.broadcasted_iota(jnp.int32, (128, 128), 1)
    row = lax.broadcasted_iota(jnp.int32, (128, 128), 0)
    k2 = lax.shift_right_logical(lane, 2) & 15
    top_band = k2 == 8

    def spare(r, drop):
        group = r - (drop == 0)
        group = group + (group > 7)
        return group, 32 - 4 * group

    def packed(x, dropped, r, drop):
        return jnp.where(top_band, pltpu.roll(dropped, spare(r, drop)[1] % 128, 1), x)

    def unpacked(blocks, drop):
        dropped = jnp.zeros((128, 128), F32)
        for r in range(16):
            if r != drop:
                group, shift = spare(r, drop)
                moved = pltpu.roll(rows_of(blocks, r, drop), -shift % 128, 1)
                dropped = jnp.where(k2 == group, moved, dropped)
        return dropped

    def rows_of(blocks, r, drop):
        return blocks[r // 8][pl.ds(r % 8 - (drop == 0 and r < 8), 128, stride=8), :]

    def put_rows(blocks, r, x, drop):
        blocks[r // 8][pl.ds(r % 8 - (drop == 0 and r < 8), 128, stride=8), :] = x

    def with_first(spec, first):
        top = lax.broadcasted_iota(jnp.int32, (8, 256), 0)
        head8 = jnp.where(top == 0, jnp.broadcast_to(first[:1], (8, 256)), spec[:8])
        return jnp.concatenate([head8, spec[8:]], axis=0)

    for i in (4, 5, 6):
        loads[i].wait()
    for h in range(2):
        for g in range(2):
            lo = h * 512 + g * 256
            error = mm(normed[...], head[:, lo : lo + 256]) - targ[:, lo : lo + 256].astype(F32)
            ab = left(tm_hi[...], tm_lo[...], error)
            for pr in range(2):
                r = h * 8 + g * 4 + pr * 2
                a = ab[:128, pr * 128 : pr * 128 + 128]
                b = ab[128:, pr * 128 : pr * 128 + 128]
                a, b = a * xc[...] - b * xs[...], b * xc[...] + a * xs[...]
                both = jnp.concatenate([a, b], axis=1)
                spec = with_first(times(both, m_hi[...], m_lo[...]), times(both[:8], s_hi[...], s_lo[...]))
                for i in range(2):
                    part = spec[:, i * 128 : i * 128 + 128]
                    own[r + i] = part
                    if r + i == 0:
                        zeroth = part
                    else:
                        put_rows(sends, r + i, packed(part, zeroth, r + i, 0), 0)
        recvs[h][mine, :] = sends[h][mine, :]
        if h == 0:
            pl.semaphore_wait(barrier, N)

            @pl.when(late)
            def _():
                pl.semaphore_wait(go, 1)

        scatter(sends[h], recvs[h], fsend.at[h], frecv.at[h], 7 + h)

    loads[7].wait()
    loads[8].wait()
    band_x = jnp.where(k2 < 8, 2 * k2, 31 - 2 * k2)
    band_x = jnp.where((lane & 1) + k2 * 2 + me * 64 == 1, NBIN - 1, band_x)
    sign = jnp.where(lane < 64, 1.0, -1.0).astype(F32)

    @pl.loop(0, 16)
    def _(jb):
        ky = jb * 8 + (row & 7) + lax.shift_right_logical(row, 3) * 128
        band_y = lax.shift_right_logical(jnp.minimum(ky, 2048 - ky), 6)
        band = jnp.minimum(jnp.maximum(band_y, band_x), NBIN - 1)
        value = jnp.zeros((128, 128), F32)
        for i in range(NBIN):
            value = jnp.where(band == i, level[i].astype(F32), value)
        wt[jb] = jnp.where(top_band, 0.0, value * 0.125)

    level_top = level[NBIN - 1].astype(F32) * 0.125
    acc = jnp.zeros((8, 128), F32)
    for r in range(16):
        part = jnp.where(top_band, own[r], 0.0)
        scaled = level_top * part
        own[r] = scaled
        acc = acc + jnp.sum((scaled * part).reshape(16, 8, 128), axis=0)

    await_all(sends[0], fsend.at[0], 7)

    @pl.when(jnp.logical_not(late))
    def _():
        pl.semaphore_signal(go, inc=1, device_id=twin, device_id_type=MESH)

    await_all(sends[1], fsend.at[1], 8)

    def swap(x):
        return pltpu.roll(x, 64, 1) * sign[: x.shape[0]]

    def outward(r, xs2):
        pq = stacked(fa_hi[...], fa_lo[...], jnp.concatenate(xs2, axis=1))
        for i in range(len(xs2)):
            p = pq[:128, i * 128 : i * 128 + 128]
            q = pq[128:, i * 128 : i * 128 + 128]
            c, s = ca[r + i], sa[r + i]
            u[r + i] = (c * p - s * q) + swap(c * q + s * p)

    await_all(recvs[0], frecv.at[0], 7)
    for r in range(2, 8, 2):
        outward(r, [rows_of(recvs, r, 0), rows_of(recvs, r + 1, 0)])
    await_all(recvs[1], frecv.at[1], 8)
    outward(0, [unpacked(recvs, 0), rows_of(recvs, 1, 0)])
    for r in range(8, 16, 2):
        outward(r, [rows_of(recvs, r, 0), rows_of(recvs, r + 1, 0)])

    def middle(jb, acc):
        at = [pl.ds(jb * 16 + i * 8, 8) for i in range(2)]
        x = jnp.concatenate([u[:, at[i], :].reshape(128, 128) for i in range(2)], axis=1)
        pq = stacked(fb_hi[...], fb_lo[...], x)
        vs = []
        for i in range(2):
            v = pq[:128, i * 128 : i * 128 + 128] + swap(pq[128:, i * 128 : i * 128 + 128])
            wv = wt[jb * 2 + i] * v
            acc = acc + jnp.sum((wv * v).reshape(16, 8, 128), axis=0)
            vs.append(wv)
        pq = stacked(fb_hi[...], fb_lo[...], jnp.concatenate(vs, axis=1))
        for i in range(2):
            p = pq[:128, i * 128 : i * 128 + 128]
            q = pq[128:, i * 128 : i * 128 + 128]
            c, s = ca[:, at[i], :].reshape(128, 128), sa[:, at[i], :].reshape(128, 128)
            u[:, at[i], :] = ((c * p - s * q) - swap(c * q + s * p)).reshape(16, 8, 128)
        return acc

    for jb in range(8):
        acc = middle(jb, acc)

    part1[pl.ds(pl.multiple_of(mz * 8, 8), 8), :] = acc

    @pl.loop(1, ZR)
    def _(p):
        pltpu.make_async_remote_copy(
            src_ref=part1.at[pl.ds(pl.multiple_of(mz * 8, 8), 8)],
            dst_ref=part1.at[pl.ds(pl.multiple_of(mz * 8, 8), 8)],
            send_sem=lsend.at[0],
            recv_sem=lrecv.at[0],
            device_id={"seq": mq * ZR + lax.rem(mz + p, ZR)},
            device_id_type=MESH,
        ).start()

    last = None
    for r in (14, 0, 2, 4, 6, 8, 10, 12):
        pq = stacked(fa_hi[...], fa_lo[...], jnp.concatenate([u[r], u[r + 1]], axis=1))
        columns = []
        for i in range(2):
            p = pq[:128, i * 128 : i * 128 + 128]
            q = pq[128:, i * 128 : i * 128 + 128]
            columns.append(p - swap(q))
        if r == 14:
            last = columns[1]
        for i in range(2):
            if r + i != 15:
                put_rows(backs, r + i, packed(columns[i], last, r + i, 15), 15)
        if r == 6 or r == 12:
            h = r // 8
            homes[h][mine, :] = backs[h][mine, :]
            scatter(backs[h], homes[h], bsend.at[h], brecv.at[h], 8 - h, h == 1)

    near = part1.at[pl.ds(0, (ZR - 1) * 8)]
    pltpu.make_async_copy(near, near, lsend.at[0]).wait()
    pltpu.make_async_copy(near, near, lrecv.at[0]).wait()
    part2[pl.ds(pl.multiple_of(mq * 8, 8), 8), :] = jnp.sum(part1[...].reshape(ZR, 8, 128), axis=0)

    @pl.loop(1, QR)
    def _(p):
        pltpu.make_async_remote_copy(
            src_ref=part2.at[pl.ds(pl.multiple_of(mq * 8, 8), 8)],
            dst_ref=part2.at[pl.ds(pl.multiple_of(mq * 8, 8), 8)],
            send_sem=lsend.at[1],
            recv_sem=lrecv.at[1],
            device_id={"seq": lax.rem(mq + p, QR) * ZR + mz},
            device_id_type=MESH,
        ).start()

    saves = []

    def home_row(r):
        return jnp.where(top_band, own[r], unpacked(homes, 15) if r == 15 else rows_of(homes, r, 15))

    def inward(g):
        blocks = []
        for pr in range(2):
            r = g * 4 + pr * 2
            x = jnp.concatenate([home_row(r), home_row(r + 1)], axis=1)
            flip = ((1,), (1,))
            spec = with_first(times(x, m_hi[...], m_lo[...], flip), times(x[:8], s_hi[...], s_lo[...], flip))
            a, b = spec[:, :128], spec[:, 128:]
            blocks.append(jnp.concatenate([a * xc[...] + b * xs[...], b * xc[...] - a * xs[...]], axis=0))
        grad = left(tm_hi[...], tm_lo[...], jnp.concatenate(blocks, axis=1), ((0,), (0,)))
        lo = g * 256
        out[:, lo : lo + 256] = grad
        saves.append(
            pltpu.make_async_copy(out.at[:, pl.ds(lo, 256)], out_h.at[:, pl.ds(lo, 256)], save.at[g])
        )
        saves[-1].start()

    for h in range(2):
        await_all(homes[h], brecv.at[h], 8 - h)
        for g in range(2):
            inward(h * 2 + g)

    far = part2.at[pl.ds(0, (QR - 1) * 8)]
    pltpu.make_async_copy(far, far, lsend.at[1]).wait()
    pltpu.make_async_copy(far, far, lrecv.at[1]).wait()
    loss[0] = jnp.sum(part2[...])
    for h in range(2):
        await_all(backs[h], bsend.at[h], 8 - h)
    for copy in saves:
        copy.wait()


def shards(features, norm_gain, pred_weight, target, patch_mask, band_level):
    plain, first = pixel_tables()
    outer, inner, ca, sa = row_tables()
    outer_hi, outer_lo = doubled(outer)
    inner_hi, inner_lo = doubled(inner)
    mats = np.stack([
        *halves(token_table()), *halves(plain), *halves(first), outer_hi, inner_hi,
        np.concatenate([outer_lo, inner_lo], axis=1),
    ])
    tables = [mats, np.stack(pixel_turn()), np.stack([ca, sa])]
    hbm = pl.BlockSpec(memory_space=pltpu.HBM)
    dma = pltpu.SemaphoreType.DMA
    block = pltpu.VMEM((N * 8, 128), F32)
    grad, loss = pl.pallas_call(
        kernel,
        out_shape=(jax.ShapeDtypeStruct((TOK, PIX), F32), jax.ShapeDtypeStruct((1,), F32)),
        in_specs=[hbm] * (6 + len(tables)),
        out_specs=(hbm, pl.BlockSpec(memory_space=pltpu.SMEM)),
        scratch_shapes=[
            pltpu.VMEM((TOK, D), BF16),
            pltpu.VMEM((D,), F32),
            pltpu.VMEM((D, PIX), BF16),
            pltpu.VMEM((TOK, PIX), BF16),
            pltpu.VMEM((1, TOK), jnp.int32),
            pltpu.SMEM((NBIN,), jnp.int32),
            pltpu.VMEM((9, 256, 256), BF16),
            pltpu.VMEM((2, 128, 128), F32),
            pltpu.VMEM((2, 16, 128, 128), F32),
            pltpu.VMEM((TOK, D), BF16),
            pltpu.VMEM((TOK, TOK), BF16),
            pltpu.VMEM((TOK, TOK), BF16),
            *[block] * 8,
            pltpu.VMEM((16, 128, 128), F32),
            pltpu.VMEM((16, 128, 128), F32),
            pltpu.VMEM((ZR * 8, 128), F32),
            pltpu.VMEM((QR * 8, 128), F32),
            pltpu.VMEM((TOK, PIX), F32),
            pltpu.VMEM((16, 128, 128), F32),
            dma((9,)),
            dma((4,)),
            pltpu.SemaphoreType.REGULAR,
            *[dma((2,))] * 6,
        ],
        compiler_params=pltpu.CompilerParams(
            collective_id=0, has_side_effects=True, vmem_limit_bytes=60 * 2**20
        ),
    )(
        features, norm_gain, pred_weight, target, patch_mask.reshape(1, TOK), band_level,
        *[jnp.asarray(table) for table in tables],
    )
    return grad * 2.0, loss * (1.0 / 33554432.0)


def solution(mesh):
    in_specs = (
        P(("scene", "seq"), None),
        P(),
        P(),
        P(("scene", "seq"), None),
        P(("scene", "seq")),
        P(),
    )
    out_specs = (P(("scene", "seq"), None), P("scene"))
    return jax.shard_map(shards, mesh=mesh, in_specs=in_specs, out_specs=out_specs, check_vma=False)
```
